256 devices in a mesh: dp: 64 (over z, x, y_lo), tensor: 4 (over y_hi, core).
Axes of the slice: x: 4, y: 4 (y_hi: 2, y_lo: 2; y = y_hi * 2 + y_lo), z: 8, core: 2. Of those that a mesh axis runs over, the one named last changes fastest.
Arguments:
- tokens: bfloat16 [32768, 8192], P('dp'), may hold values from -6 to 6
- grad_out: bfloat16 [32768, 8192], P('dp', 'tensor'), may hold values from -0.015625 to 0.015625
- basis: bfloat16 [8192, 512], P(('dp', 'tensor')), may hold values from -0.5 to 0.5
- first_moment: float32 [512, 8192], P('dp', 'tensor'), may hold values from -0.3 to 0.3
- second_moment: float32 [512, 8192], P('dp', 'tensor'), may hold values from 0.02 to 0.2
Outputs:
- update: bfloat16 [8192, 8192], P('dp', 'tensor')
- new_first: float32 [512, 8192], P('dp', 'tensor')
- new_second: float32 [512, 8192], P('dp', 'tensor')
The draws below stay inside these ranges and needn't reach their ends.
All inputs are finite; a program needn't handle non-finite values.
Results may differ from the reference program's by a relative error of at most 0.006.
Values may be sent and summed in bfloat16 or wider, within the bound.
No kernel may reach another device: no remote copies, remote signals or barrier semaphores. Data moves between devices by JAX's collectives and lax.ppermute only.
A program may use at most 64 MiB of HBM per device.

```python
import math
import jax
import jax.numpy as jnp

D = 8192
QW = 8192
R = 512
STEP = 20
TOKENS = 32768


def spiked(entries, stream_key, source, target, blocks, factor):
    owner, partner = [(jnp.arange(entries.shape[dim]) // (entries.shape[dim] // blocks)).reshape([-1 if axis == dim else 1 for axis in range(entries.ndim)]) for dim in (source, target)]
    chosen = jax.random.permutation(stream_key, blocks)[partner]
    strong = (owner == chosen) | (owner == (partner + blocks // 2) % blocks)
    return jnp.where(strong, factor * entries, entries)


def block_levels(own_key, dims, pieces, smallest, largest):
    gain, own = 1.0, jax.random.fold_in(own_key, 6)
    for dim, shards_of in pieces:
        draws = jnp.exp(jax.random.uniform(jax.random.fold_in(own, dim), (shards_of,), jnp.float32, smallest / len(pieces), largest / len(pieces)))
        gain = gain * jnp.repeat(draws, dims[dim] // shards_of).reshape([-1 if axis == dim else 1 for axis in range(len(dims))])
    return gain


def bell_draw(rng, shape, scale, bound, cuts=(), kind=jnp.bfloat16):
    array = scale * jax.random.normal(rng, shape, jnp.float32)
    if cuts:
        array = array * block_levels(rng, shape, cuts, -0.22, 0.18)
    return jnp.clip(array, -bound, bound).astype(kind)


def bell_draw_with(own_key, shape, spread, reach, pieces, heavy, kind=jnp.bfloat16):
    result = spread * jax.random.normal(own_key, shape, jnp.float32)
    if pieces:
        result = result * block_levels(own_key, shape, pieces, -0.22, 0.18)
    return jnp.clip(spiked(result, jax.random.fold_in(own_key, 3), *heavy), -reach, reach).astype(kind)


def setup_inputs(seed: int = 0) -> dict:
    splits = jax.random.split(jax.random.key(seed), 6)
    tokens = bell_draw(splits[0], (TOKENS, D), 1.0, 6.0, ((0, 64),))
    grad_out = bell_draw_with(splits[1], (TOKENS, QW), 0.0009765625, 0.015625, ((0, 64), (1, 4)), (0, 1, 64, 4.0))
    basis = bell_draw(splits[2], (D, R), (R // 4) ** -0.5, 0.5, ((0, 256),))
    first_moment = bell_draw(splits[3], (R, QW), 0.05, 0.3, ((0, 64), (1, 4)), jnp.float32)
    second_moment = jnp.clip(jnp.exp(math.log(0.2) - 2.3025851 * jax.random.uniform(splits[4], (R, QW), jnp.float32) ** block_levels(splits[4], (R, QW), ((0, 64), (1, 4)), -0.2, 0.2)), 0.02, 0.2)
    return {"tokens": tokens, "grad_out": grad_out, "basis": basis, "first_moment": first_moment, "second_moment": second_moment}


def reference(tokens, grad_out, basis, first_moment, second_moment):
    coords = jnp.dot(tokens, basis, preferred_element_type=jnp.float32).astype(jnp.bfloat16)
    projected = jnp.dot(coords.T, grad_out, preferred_element_type=jnp.float32)
    new_first = 0.9 * first_moment + 0.1 * projected
    new_second = 0.95 * second_moment + 0.05 * projected * projected
    first_fix = 1.0 - 0.9 ** STEP
    second_fix = 1.0 - 0.95 ** STEP
    step_dir = (new_first / first_fix / (jnp.sqrt(new_second / second_fix) + 1e-08)).astype(jnp.bfloat16)
    update = jnp.dot(basis, step_dir, preferred_element_type=jnp.float32).astype(jnp.bfloat16)
    return (update, new_first, new_second)
```

```python
import jax
import jax.numpy as jnp
from jax import lax
from jax.sharding import Mesh, PartitionSpec as P

STEP = 20
AXES = ("z", "x", "yl", "yh", "core")
DP = ("z", "x", "yl")
TENSOR = ("yh", "core")
PLANE = ("x", "yl")
NZ, NX, NYL, NYH, NC = 8, 4, 2, 2, 2
NP = NX * NYL
NT = NYH * NC


def exchange(blocks, axes):
    return lax.all_to_all(blocks, axes, 0, 0, tiled=True)


def local(tokens, grad_out, basis, first_moment, second_moment):
    f32, bf16 = jnp.float32, jnp.bfloat16
    rows, rank = basis.shape
    quarter = rank // NT
    dim = tokens.shape[1]
    columns = grad_out.shape[1]
    own = rank // (NZ * NP)

    pieces = basis.reshape(rows, NT, quarter).transpose(1, 0, 2)
    pieces = jnp.broadcast_to(pieces[None], (NZ, NT, rows, quarter))
    line = exchange(pieces.reshape(NZ * NT, rows, quarter), ("z",) + TENSOR)
    plane = exchange(jnp.broadcast_to(line[None], (NP,) + line.shape), PLANE)
    basis_part = plane.reshape(NP, NZ, NT * rows, quarter).transpose(1, 0, 2, 3).reshape(dim, quarter)

    coords = jnp.dot(tokens, basis_part, preferred_element_type=f32).astype(bf16)
    coords = lax.all_gather(coords.T, TENSOR, axis=0, tiled=True)

    coords = coords.reshape(NZ, NP, own, -1).transpose(1, 0, 2, 3).reshape(rank, -1)
    partial = jnp.dot(coords, grad_out, preferred_element_type=f32).astype(bf16)
    partial = exchange(partial.reshape(NP, NZ * own, columns), PLANE)
    partial = jnp.sum(partial.astype(f32), axis=0).astype(bf16)
    partial = exchange(partial.reshape(NZ, own, columns), ("z",))
    projected = jnp.sum(partial.astype(f32), axis=0)

    new_first = 0.9 * first_moment + 0.1 * projected
    new_second = 0.95 * second_moment + 0.05 * projected * projected
    first_fix = 1.0 - 0.9**STEP
    second_fix = 1.0 - 0.95**STEP
    step_dir = (new_first / first_fix / (jnp.sqrt(new_second / second_fix) + 1e-08)).astype(bf16)

    line = exchange(jnp.broadcast_to(step_dir[None], (NZ, own, columns)), ("z",))
    plane = exchange(jnp.broadcast_to(line[None], (NP,) + line.shape), PLANE)
    rows_here = lax.all_gather(basis, TENSOR, axis=0, tiled=True)
    rows_here = rows_here.reshape(-1, NZ, NP, own).transpose(0, 2, 1, 3).reshape(-1, rank)
    update = jnp.dot(rows_here, plane.reshape(rank, columns), preferred_element_type=f32)
    return (update.astype(bf16), new_first, new_second)


def solution(mesh):
    fine = Mesh(mesh.devices.reshape(NZ, NX, NYL, NYH, NC), AXES)
    placed = (
        P(DP, None),
        P(DP, TENSOR),
        P(DP + TENSOR, None),
        P(DP, TENSOR),
        P(DP, TENSOR),
    )
    return jax.shard_map(
        local,
        mesh=fine,
        in_specs=placed,
        out_specs=(P(DP, TENSOR), P(DP, TENSOR), P(DP, TENSOR)),
        check_vma=False,
    )
```

```python
import jax
import jax.numpy as jnp
from jax import lax
from jax.experimental import pallas as pl
from jax.experimental.pallas import tpu as pltpu
from jax.sharding import Mesh, PartitionSpec as P

STEP = 20
AXES = ("z", "x", "yl", "yh", "core")
DP = ("z", "x", "yl")
TENSOR = ("yh", "core")
PLANE = ("x", "yl")
NZ, NX, NYL, NYH, NC = 8, 4, 2, 2, 2
NP = NX * NYL
NT = NYH * NC
MIB = 1024 * 1024
F32, BF16 = jnp.float32, jnp.bfloat16


def exchange(blocks, axes):
    return lax.all_to_all(blocks, axes, 0, 0, tiled=True)


def gather(block, axes, members):
    return exchange(jnp.broadcast_to(block[None], (members,) + block.shape), axes)


def swap(block, axis):
    return lax.ppermute(block, axis, ((0, 1), (1, 0)))


def peers(block):
    far = swap(block, "yh")
    return block, swap(block, "core"), far, swap(far, "core")


def halves(value):
    high = value.astype(BF16)
    return high, (value - high.astype(F32)).astype(BF16)


def call(kernel, index, grid, in_specs, out_specs, out_shape, scratch, cost, limit, *args):
    return pl.pallas_call(
        kernel,
        grid_spec=pltpu.PrefetchScalarGridSpec(
            num_scalar_prefetch=1,
            grid=grid,
            in_specs=in_specs,
            out_specs=out_specs,
            scratch_shapes=scratch,
        ),
        out_shape=out_shape,
        compiler_params=pltpu.CompilerParams(vmem_limit_bytes=limit * MIB),
        cost_estimate=pl.CostEstimate(flops=cost[0], bytes_accessed=cost[1], transcendentals=0),
    )(index, *args)


def quarter_copies(index, pieces):
    rows, rank = pieces[0].shape
    quarter = rank // NT
    group = NT * rows

    def kernel(index_ref, *refs):
        out = refs[-1]
        for k in range(NT):
            start = pl.multiple_of((index_ref[0] ^ k) * rows, rows)
            for z in range(NZ):
                out[z, pl.ds(start, rows), :] = refs[k][...]

    return call(
        kernel,
        index,
        (1,),
        [pl.BlockSpec((rows, quarter), lambda i, t: (0, t[0]))] * NT,
        pl.BlockSpec((NZ, group, quarter), lambda i, t: (0, 0, 0)),
        jax.ShapeDtypeStruct((NZ, group, quarter), BF16),
        [],
        (0, 2 * NZ * group * quarter),
        16,
        *pieces,
    )


def coordinates(tokens, plane):
    part = plane.transpose(1, 0, 2, 3).reshape(tokens.shape[1], plane.shape[3])
    return jnp.dot(tokens, part, preferred_element_type=F32).astype(BF16).T


def partial_sums(index, coords, grad_out, first_moment, second_moment):
    quarter, count = coords[0].shape
    rank, columns = NT * quarter, grad_out.shape[1]
    own, part = first_moment.shape[0], columns // NP
    rows = rank + 4 * own

    def kernel(index_ref, *refs):
        pieces, (grad_ref, first_ref, second_ref, out) = refs[:NT], refs[NT:]
        for k in range(NT):
            start = pl.multiple_of((index_ref[0] ^ k) * quarter, quarter)
            out[0, pl.ds(start, quarter), :] = jnp.dot(
                pieces[k][...], grad_ref[...], preferred_element_type=F32
            ).astype(BF16)
        out[0, rank : rank + 2 * own, :] = jnp.concatenate(halves(first_ref[...]))
        out[0, rank + 2 * own :, :] = jnp.concatenate(halves(second_ref[...]))

    return call(
        kernel,
        index,
        (NP,),
        [pl.BlockSpec((quarter, count), lambda p, t: (0, 0))] * NT
        + [pl.BlockSpec((count, part), lambda p, t: (0, p))]
        + [pl.BlockSpec((own, part), lambda p, t: (0, p))] * 2,
        pl.BlockSpec((1, rows, part), lambda p, t: (p, 0, 0)),
        jax.ShapeDtypeStruct((NP, rows, part), BF16),
        [],
        (2 * rank * count * columns, 2 * columns * (count + rows)),
        24,
        *coords,
        grad_out,
        first_moment,
        second_moment,
    )


def plane_sums(index, received, own):
    members, rows, part = received.shape
    rank = rows - 4 * own
    step = rank // 4

    def kernel(index_ref, sums_ref, moments_ref, out, first, second):
        total = sums_ref[0].astype(F32)
        for source in range(1, members):
            total += sums_ref[source].astype(F32)
        out[...] = total.astype(BF16)

        @pl.when(pl.program_id(0) == 0)
        def _():
            for source in range(members):
                block = moments_ref[source].astype(F32)
                here = slice(source * own, (source + 1) * own)
                first[here, :] = block[:own] + block[own : 2 * own]
                second[here, :] = block[2 * own : 3 * own] + block[3 * own :]

    return call(
        kernel,
        index,
        (4,),
        [
            pl.BlockSpec((members, step, part), lambda i, t: (0, i, 0)),
            pl.BlockSpec((members, 4 * own, part), lambda i, t: (0, rank // (4 * own), 0)),
        ],
        [
            pl.BlockSpec((step, part), lambda i, t: (i, 0)),
            pl.BlockSpec((members * own, part), lambda i, t: (0, 0)),
            pl.BlockSpec((members * own, part), lambda i, t: (0, 0)),
        ],
        [
            jax.ShapeDtypeStruct((rank, part), BF16),
            jax.ShapeDtypeStruct((members * own, part), F32),
            jax.ShapeDtypeStruct((members * own, part), F32),
        ],
        [],
        (members * rank * part, 2 * members * rows * part),
        24,
        received,
        received,
    )


def update_blocks(index, pieces, step_dir, projected, own):
    quarter = pieces[0].shape[1]
    group = pieces[0].shape[0] // NP
    part = step_dir.shape[1]

    def kernel(index_ref, *refs):
        blocks, (step_ref, projected_ref, out) = refs[:NT], refs[NT:]
        total = 0.0
        for k in range(NT):
            start = pl.multiple_of((index_ref[0] ^ k) * quarter, quarter)
            total += jnp.dot(
                blocks[k][...], step_ref[pl.ds(start, quarter), :], preferred_element_type=F32
            )
        out[0, :group, :] = total.astype(BF16)
        out[0, group:, :] = jnp.concatenate(halves(projected_ref[...]))

    return call(
        kernel,
        index,
        (NP,),
        [pl.BlockSpec((group, quarter), lambda p, t: (p, 0))] * NT
        + [
            pl.BlockSpec((NT * quarter, part), lambda p, t: (0, 0)),
            pl.BlockSpec((own, part), lambda p, t: (p, 0)),
        ],
        pl.BlockSpec((1, group + 2 * own, part), lambda p, t: (p, 0, 0)),
        jax.ShapeDtypeStruct((NP, group + 2 * own, part), BF16),
        [],
        (2 * NP * group * NT * quarter * part, 2 * NP * group * (NT * quarter + part)),
        24,
        *pieces,
        step_dir,
        projected,
    )


def moments_of(first_moment, second_moment, projected):
    new_first = 0.9 * first_moment + 0.1 * projected
    new_second = 0.95 * second_moment + 0.05 * projected * projected
    return new_first, new_second


def local(tokens, grad_out, basis, first_moment, second_moment):
    rows, rank = basis.shape
    quarter = rank // NT
    group = NT * rows
    columns = grad_out.shape[1]
    own = rank // (NZ * NP)
    part = columns // NP
    index = (NC * lax.axis_index("yh") + lax.axis_index("core")).astype(jnp.int32).reshape(1)

    line = exchange(quarter_copies(index, peers(basis)), ("z",))
    plane = gather(line, PLANE, NP)
    coords = peers(coordinates(tokens, plane))

    partial = partial_sums(index, coords, grad_out, first_moment, second_moment)
    partial, first_part, second_part = plane_sums(index, exchange(partial, PLANE), own)

    plane, partial = lax.optimization_barrier((plane, partial))
    rows_here = lax.dynamic_index_in_dim(plane, lax.axis_index("z"), axis=1, keepdims=False)
    rows_here = peers(rows_here.reshape(NP * group, quarter))

    partial = exchange(partial.reshape(NZ, NP * own, part), ("z",))
    projected = jnp.sum(partial.astype(F32), axis=0)
    new_first, new_second = moments_of(first_part, second_part, projected)
    first_fix = 1.0 - 0.9**STEP
    second_fix = 1.0 - 0.95**STEP
    step_dir = (new_first / first_fix / (jnp.sqrt(new_second / second_fix) + 1e-08)).astype(BF16)
    step_dir = gather(step_dir, ("z",), NZ).reshape(rank, part)

    back = update_blocks(index, rows_here, step_dir, projected, own)
    back = exchange(back, PLANE).transpose(1, 0, 2).reshape(group + 2 * own, columns)
    projected = back[group : group + own].astype(F32) + back[group + own :].astype(F32)
    new_first, new_second = moments_of(first_moment, second_moment, projected)
    return (back[:group], new_first, new_second)


def solution(mesh):
    fine = Mesh(mesh.devices.reshape(NZ, NX, NYL, NYH, NC), AXES)
    placed = (
        P(DP, None),
        P(DP, TENSOR),
        P(DP + TENSOR, None),
        P(DP, TENSOR),
        P(DP, TENSOR),
    )
    return jax.shard_map(
        local,
        mesh=fine,
        in_specs=placed,
        out_specs=(P(DP, TENSOR), P(DP, TENSOR), P(DP, TENSOR)),
        check_vma=False,
    )
```

```python
import jax
import jax.numpy as jnp
from jax import lax
from jax.experimental import pallas as pl
from jax.experimental.pallas import tpu as pltpu
from jax.sharding import Mesh, PartitionSpec as P

STEP = 20
AXES = ("z", "x", "yl", "yh", "core")
DP = ("z", "x", "yl")
TENSOR = ("yh", "core")
PLANE = ("x", "yl")
NZ, NX, NYL, NYH, NC = 8, 4, 2, 2, 2
NP = NX * NYL
NT = NYH * NC
MIB = 1024 * 1024
F32, BF16 = jnp.float32, jnp.bfloat16


def exchange(blocks, axes):
    return lax.all_to_all(blocks, axes, 0, 0, tiled=True)


def gather(block, axes, members):
    return exchange(jnp.broadcast_to(block[None], (members,) + block.shape), axes)


def swap(block, axis):
    return lax.ppermute(block, axis, ((0, 1), (1, 0)))


def peers(block):
    far = swap(block, "yh")
    return block, swap(block, "core"), far, swap(far, "core")


def halves(value):
    high = value.astype(BF16)
    return high, (value - high.astype(F32)).astype(BF16)


def call(kernel, index, grid, in_specs, out_specs, out_shape, scratch, cost, limit, *args):
    return pl.pallas_call(
        kernel,
        grid_spec=pltpu.PrefetchScalarGridSpec(
            num_scalar_prefetch=1,
            grid=grid,
            in_specs=in_specs,
            out_specs=out_specs,
            scratch_shapes=scratch,
        ),
        out_shape=out_shape,
        compiler_params=pltpu.CompilerParams(vmem_limit_bytes=limit * MIB),
        cost_estimate=pl.CostEstimate(flops=cost[0], bytes_accessed=cost[1], transcendentals=0),
    )(index, *args)


def along(block, shift):
    return lax.ppermute(block, "x", [(i, (i + shift) % NX) for i in range(NX)])


def plane_blocks(line):
    half = line.shape[0] // 2
    low, high = line[:half], line[half:]
    beside = swap(line, "yl")
    left_low, right_high = along(low, 1), along(high, -1)
    left_high, right_low = along(high, 1), along(low, -1)
    far_low, far_high = along(left_low, 1), along(right_high, -1)
    beside_left, beside_right = along(beside, 1), along(beside, -1)
    pieces = (
        (line, 0, 0, 0),
        (beside, 0, 1, 0),
        (left_low, NX - 1, 0, 0),
        (left_high, NX - 1, 0, half),
        (right_low, 1, 0, 0),
        (right_high, 1, 0, half),
        (far_low, 2, 0, 0),
        (far_high, 2, 0, half),
        (beside_left, NX - 1, 1, 0),
        (beside_right, 1, 1, 0),
        (swap(far_low, "yl"), 2, 1, 0),
        (swap(far_high, "yl"), 2, 1, half),
    )
    place = jnp.stack([lax.axis_index("x"), lax.axis_index("yl")]).astype(jnp.int32)

    def kernel(place_ref, *refs):
        out, arrived = refs[-2:]
        copies = []
        for k, (ref, (_, dx, dy, start)) in enumerate(zip(refs, pieces)):
            member = ((place_ref[0] + dx) & (NX - 1)) * NYL + (place_ref[1] ^ dy)
            to = out.at[pl.ds(start, ref.shape[0]), member]
            copies.append(pltpu.make_async_copy(ref, to, arrived.at[k]))
        for copy in copies:
            copy.start()
        for copy in copies:
            copy.wait()

    blocks = pl.pallas_call(
        kernel,
        in_specs=[pl.BlockSpec(memory_space=pltpu.SMEM)]
        + [pl.BlockSpec(memory_space=pl.ANY)] * len(pieces),
        out_specs=pl.BlockSpec(memory_space=pltpu.VMEM),
        out_shape=jax.ShapeDtypeStruct((line.shape[0], NP) + line.shape[1:], BF16),
        scratch_shapes=[pltpu.SemaphoreType.DMA((len(pieces),))],
        compiler_params=pltpu.CompilerParams(vmem_limit_bytes=24 * MIB),
        cost_estimate=pl.CostEstimate(flops=0, bytes_accessed=4 * NP * line.size, transcendentals=0),
    )(place, *(piece[0] for piece in pieces))
    return blocks, beside


def loaded(array):
    def kernel(source, out, arrived):
        copy = pltpu.make_async_copy(source, out, arrived)
        copy.start()
        copy.wait()

    return pl.pallas_call(
        kernel,
        in_specs=[pl.BlockSpec(memory_space=pltpu.HBM)],
        out_specs=pl.BlockSpec(memory_space=pltpu.VMEM),
        out_shape=jax.ShapeDtypeStruct(array.shape, array.dtype),
        scratch_shapes=[pltpu.SemaphoreType.DMA],
        compiler_params=pltpu.CompilerParams(vmem_limit_bytes=24 * MIB),
        cost_estimate=pl.CostEstimate(flops=0, bytes_accessed=4 * array.size, transcendentals=0),
    )(array)

def coordinates(tokens, blocks):
    part = blocks.reshape(tokens.shape[1], blocks.shape[3])
    return jnp.dot(tokens, part, preferred_element_type=F32).astype(BF16).T


def partial_sums(index, coords, grad_out, first_moment, second_moment):
    quarter, count = coords[0].shape
    rank, columns = NT * quarter, grad_out.shape[1]
    own, part = first_moment.shape[0], columns // NP
    rows = rank + 4 * own

    def kernel(index_ref, *refs):
        pieces, (grad_ref, first_ref, second_ref, out) = refs[:NT], refs[NT:]
        for k in range(NT):
            start = pl.multiple_of((index_ref[0] ^ k) * quarter, quarter)
            out[0, pl.ds(start, quarter), :] = jnp.dot(
                pieces[k][...], grad_ref[...], preferred_element_type=F32
            ).astype(BF16)
        out[0, rank : rank + 2 * own, :] = jnp.concatenate(halves(first_ref[...]))
        out[0, rank + 2 * own :, :] = jnp.concatenate(halves(second_ref[...]))

    return call(
        kernel,
        index,
        (NP,),
        [pl.BlockSpec((quarter, count), lambda p, t: (0, 0))] * NT
        + [pl.BlockSpec((count, part), lambda p, t: (0, p))]
        + [pl.BlockSpec((own, part), lambda p, t: (0, p))] * 2,
        pl.BlockSpec((1, rows, part), lambda p, t: (p, 0, 0)),
        jax.ShapeDtypeStruct((NP, rows, part), BF16),
        [],
        (2 * rank * count * columns, 2 * columns * (count + rows)),
        24,
        *coords,
        grad_out,
        first_moment,
        second_moment,
    )


def plane_sums(index, received, own):
    members, rows, part = received.shape
    rank = rows - 4 * own
    step = rank // 4

    def kernel(index_ref, sums_ref, moments_ref, out, first, second):
        total = sums_ref[0].astype(F32)
        for source in range(1, members):
            total += sums_ref[source].astype(F32)
        out[...] = total.astype(BF16)

        @pl.when(pl.program_id(0) == 0)
        def _():
            for source in range(members):
                block = moments_ref[source].astype(F32)
                here = slice(source * own, (source + 1) * own)
                first[here, :] = block[:own] + block[own : 2 * own]
                second[here, :] = block[2 * own : 3 * own] + block[3 * own :]

    return call(
        kernel,
        index,
        (4,),
        [
            pl.BlockSpec((members, step, part), lambda i, t: (0, i, 0)),
            pl.BlockSpec((members, 4 * own, part), lambda i, t: (0, rank // (4 * own), 0)),
        ],
        [
            pl.BlockSpec((step, part), lambda i, t: (i, 0)),
            pl.BlockSpec((members * own, part), lambda i, t: (0, 0)),
            pl.BlockSpec((members * own, part), lambda i, t: (0, 0)),
        ],
        [
            jax.ShapeDtypeStruct((rank, part), BF16),
            jax.ShapeDtypeStruct((members * own, part), F32),
            jax.ShapeDtypeStruct((members * own, part), F32),
        ],
        [],
        (members * rank * part, 2 * members * rows * part),
        24,
        received,
        received,
    )


def update_blocks(index, pieces, step_dir, projected, own):
    quarter = pieces[0].shape[1]
    group = pieces[0].shape[0] // NP
    part = step_dir.shape[1]

    def kernel(index_ref, *refs):
        blocks, (step_ref, projected_ref, out) = refs[:NT], refs[NT:]
        total = 0.0
        for k in range(NT):
            start = pl.multiple_of((index_ref[0] ^ k) * quarter, quarter)
            total += jnp.dot(
                blocks[k][...], step_ref[pl.ds(start, quarter), :], preferred_element_type=F32
            )
        out[0, :group, :] = total.astype(BF16)
        out[0, group:, :] = jnp.concatenate(halves(projected_ref[...]))

    return call(
        kernel,
        index,
        (NP,),
        [pl.BlockSpec((group, quarter), lambda p, t: (p, 0))] * NT
        + [
            pl.BlockSpec((NT * quarter, part), lambda p, t: (0, 0)),
            pl.BlockSpec((own, part), lambda p, t: (p, 0)),
        ],
        pl.BlockSpec((1, group + 2 * own, part), lambda p, t: (p, 0, 0)),
        jax.ShapeDtypeStruct((NP, group + 2 * own, part), BF16),
        [],
        (2 * NP * group * NT * quarter * part, 2 * NP * group * (NT * quarter + part)),
        24,
        *pieces,
        step_dir,
        projected,
    )


def moments_of(first_moment, second_moment, projected):
    new_first = 0.9 * first_moment + 0.1 * projected
    new_second = 0.95 * second_moment + 0.05 * projected * projected
    return new_first, new_second


def local(tokens, grad_out, basis, first_moment, second_moment):
    rows, rank = basis.shape
    quarter = rank // NT
    group = NT * rows
    columns = grad_out.shape[1]
    own = rank // (NZ * NP)
    part = columns // NP
    index = (NC * lax.axis_index("yh") + lax.axis_index("core")).astype(jnp.int32).reshape(1)

    pieces = basis.reshape(rows, NT, quarter).transpose(1, 0, 2)
    pieces = jnp.broadcast_to(pieces[None], (NZ, NT, rows, quarter))
    line = exchange(pieces.reshape(NZ * NT, rows, quarter), ("z",) + TENSOR)
    blocks, beside = plane_blocks(line.reshape(NZ, group, quarter))
    tokens, beside = lax.optimization_barrier((tokens, beside))
    tokens = loaded(tokens)
    coords = peers(coordinates(tokens, blocks))

    partial = partial_sums(index, coords, grad_out, first_moment, second_moment)
    partial, first_part, second_part = plane_sums(index, exchange(partial, PLANE), own)

    blocks, partial = lax.optimization_barrier((blocks, partial))
    rows_here = lax.dynamic_index_in_dim(blocks, lax.axis_index("z"), axis=0, keepdims=False)
    rows_here = peers(rows_here.reshape(NP * group, quarter))

    partial = exchange(partial.reshape(NZ, NP * own, part), ("z",))
    projected = jnp.sum(partial.astype(F32), axis=0)
    new_first, new_second = moments_of(first_part, second_part, projected)
    first_fix = 1.0 - 0.9**STEP
    second_fix = 1.0 - 0.95**STEP
    step_dir = (new_first / first_fix / (jnp.sqrt(new_second / second_fix) + 1e-08)).astype(BF16)
    step_dir = gather(step_dir, ("z",), NZ).reshape(rank, part)

    back = update_blocks(index, rows_here, step_dir, projected, own)
    back = exchange(back, PLANE).transpose(1, 0, 2).reshape(group + 2 * own, columns)
    projected = back[group : group + own].astype(F32) + back[group + own :].astype(F32)
    new_first, new_second = moments_of(first_moment, second_moment, projected)
    return (back[:group], new_first, new_second)


def solution(mesh):
    fine = Mesh(mesh.devices.reshape(NZ, NX, NYL, NYH, NC), AXES)
    placed = (
        P(DP, None),
        P(DP, TENSOR),
        P(DP + TENSOR, None),
        P(DP, TENSOR),
        P(DP, TENSOR),
    )
    return jax.shard_map(
        local,
        mesh=fine,
        in_specs=placed,
        out_specs=(P(DP, TENSOR), P(DP, TENSOR), P(DP, TENSOR)),
        check_vma=False,
    )
```

```python
import jax
import jax.numpy as jnp
from jax import lax
from jax.experimental import pallas as pl
from jax.experimental.pallas import tpu as pltpu
from jax.sharding import Mesh, PartitionSpec as P

STEP = 20
AXES = ("z", "x", "yl", "yh", "core")
DP = ("z", "x", "yl")
TENSOR = ("yh", "core")
PLANE = ("x", "yl")
NZ, NX, NYL, NYH, NC = 8, 4, 2, 2, 2
NP = NX * NYL
NT = NYH * NC
PAIR = 2
MIB = 1024 * 1024
F32, BF16 = jnp.float32, jnp.bfloat16


def exchange(blocks, axes):
    return lax.all_to_all(blocks, axes, 0, 0, tiled=True)


def gather(block, axes, members):
    return exchange(jnp.broadcast_to(block[None], (members,) + block.shape), axes)


def swap(block, axis):
    return lax.ppermute(block, axis, ((0, 1), (1, 0)))


def peers(block):
    far = swap(block, "yh")
    return block, swap(block, "core"), far, swap(far, "core")


def halves(value):
    high = value.astype(BF16)
    return high, (value - high.astype(F32)).astype(BF16)


def call(kernel, index, grid, in_specs, out_specs, out_shape, scratch, cost, limit, *args):
    return pl.pallas_call(
        kernel,
        grid_spec=pltpu.PrefetchScalarGridSpec(
            num_scalar_prefetch=1,
            grid=grid,
            in_specs=in_specs,
            out_specs=out_specs,
            scratch_shapes=scratch,
        ),
        out_shape=out_shape,
        compiler_params=pltpu.CompilerParams(vmem_limit_bytes=limit * MIB),
        cost_estimate=pl.CostEstimate(flops=cost[0], bytes_accessed=cost[1], transcendentals=0),
    )(index, *args)


def along(block, shift):
    return lax.ppermute(block, "x", [(i, (i + shift) % NX) for i in range(NX)])


def plane_blocks(line):
    half = line.shape[0] // 2
    beside, left, right = swap(line, "yl"), along(line, 1), along(line, -1)
    far_low, far_high = along(left[:half], 1), along(right[half:], -1)
    beside_left, beside_right = along(beside, 1), along(beside, -1)
    pieces = (
        (line, 0, 0, 0),
        (beside, 0, 1, 0),
        (left, NX - 1, 0, 0),
        (right, 1, 0, 0),
        (far_low, 2, 0, 0),
        (far_high, 2, 0, half),
        (beside_left, NX - 1, 1, 0),
        (beside_right, 1, 1, 0),
        (swap(far_low, "yl"), 2, 1, 0),
        (swap(far_high, "yl"), 2, 1, half),
    )
    x, yl = lax.axis_index("x"), lax.axis_index("yl")
    blocks = jnp.zeros((line.shape[0], NP) + line.shape[1:], BF16)
    for piece, dx, dy, start in pieces:
        member = ((x + dx) & (NX - 1)) * NYL + (yl ^ dy)
        blocks = lax.dynamic_update_slice(blocks, piece[:, None], (start, member, 0, 0))
    return blocks, beside


def loaded(*arrays):
    count = len(arrays)

    def kernel(*refs):
        sources, outs, arrived = refs[:count], refs[count:-1], refs[-1]
        copies = [
            pltpu.make_async_copy(sources[k], outs[k], arrived.at[k]) for k in range(count)
        ]
        for copy in copies:
            copy.start()
        for copy in copies:
            copy.wait()

    return pl.pallas_call(
        kernel,
        in_specs=[pl.BlockSpec(memory_space=pltpu.HBM)] * count,
        out_specs=[pl.BlockSpec(memory_space=pltpu.VMEM)] * count,
        out_shape=[jax.ShapeDtypeStruct(array.shape, array.dtype) for array in arrays],
        scratch_shapes=[pltpu.SemaphoreType.DMA((count,))],
        compiler_params=pltpu.CompilerParams(vmem_limit_bytes=40 * MIB),
        cost_estimate=pl.CostEstimate(
            flops=0, bytes_accessed=4 * sum(array.size for array in arrays), transcendentals=0
        ),
    )(*arrays)


def coordinates(tokens, blocks):
    part = blocks.reshape(tokens.shape[1], blocks.shape[3])
    return jnp.dot(tokens, part, preferred_element_type=F32).astype(BF16).T


def partial_sums(index, coords, grad_out, first_moment, second_moment):
    quarter, count = coords[0].shape
    rank, columns = NT * quarter, grad_out.shape[1]
    own, part = first_moment.shape[0], columns // NP
    rows = rank + 4 * own

    def kernel(index_ref, *refs):
        pieces, (grad_ref, first_ref, second_ref, out) = refs[:NT], refs[NT:]
        for j in range(PAIR):
            here = slice(j * part, (j + 1) * part)
            for k in range(NT):
                start = pl.multiple_of((index_ref[0] ^ k) * quarter, quarter)
                out[j, pl.ds(start, quarter), :] = jnp.dot(
                    pieces[k][...], grad_ref[:, here], preferred_element_type=F32
                ).astype(BF16)
            out[j, rank : rank + 2 * own, :] = jnp.concatenate(halves(first_ref[:, here]))
            out[j, rank + 2 * own :, :] = jnp.concatenate(halves(second_ref[:, here]))

    return call(
        kernel,
        index,
        (NP // PAIR,),
        [pl.BlockSpec((quarter, count), lambda p, t: (0, 0))] * NT
        + [pl.BlockSpec((count, PAIR * part), lambda p, t: (0, p))]
        + [pl.BlockSpec((own, PAIR * part), lambda p, t: (0, p))] * 2,
        pl.BlockSpec((PAIR, rows, part), lambda p, t: (p, 0, 0)),
        jax.ShapeDtypeStruct((NP, rows, part), BF16),
        [],
        (2 * rank * count * columns, 2 * columns * (count + rows)),
        24,
        *coords,
        grad_out,
        first_moment,
        second_moment,
    )


def plane_sums(index, received, own):
    members, rows, part = received.shape
    rank = rows - 4 * own
    step = rank // 4

    def kernel(index_ref, sums_ref, moments_ref, out, first, second):
        total = sums_ref[0].astype(F32)
        for source in range(1, members):
            total += sums_ref[source].astype(F32)
        out[...] = total.astype(BF16)

        @pl.when(pl.program_id(0) == 0)
        def _():
            for source in range(members):
                block = moments_ref[source].astype(F32)
                here = slice(source * own, (source + 1) * own)
                first[here, :] = block[:own] + block[own : 2 * own]
                second[here, :] = block[2 * own : 3 * own] + block[3 * own :]

    return call(
        kernel,
        index,
        (4,),
        [
            pl.BlockSpec((members, step, part), lambda i, t: (0, i, 0)),
            pl.BlockSpec((members, 4 * own, part), lambda i, t: (0, rank // (4 * own), 0)),
        ],
        [
            pl.BlockSpec((step, part), lambda i, t: (i, 0)),
            pl.BlockSpec((members * own, part), lambda i, t: (0, 0)),
            pl.BlockSpec((members * own, part), lambda i, t: (0, 0)),
        ],
        [
            jax.ShapeDtypeStruct((rank, part), BF16),
            jax.ShapeDtypeStruct((members * own, part), F32),
            jax.ShapeDtypeStruct((members * own, part), F32),
        ],
        [],
        (members * rank * part, 2 * members * rows * part),
        24,
        received,
        received,
    )


def update_blocks(index, pieces, step_dir, projected, own):
    quarter = pieces[0].shape[1]
    group = pieces[0].shape[0] // NP
    part = step_dir.shape[1]

    def kernel(index_ref, *refs):
        blocks, (step_ref, projected_ref, out) = refs[:NT], refs[NT:]
        total = 0.0
        for k in range(NT):
            start = pl.multiple_of((index_ref[0] ^ k) * quarter, quarter)
            total += jnp.dot(
                blocks[k][...], step_ref[pl.ds(start, quarter), :], preferred_element_type=F32
            )
        out[0, :group, :] = total.astype(BF16)
        out[0, group:, :] = jnp.concatenate(halves(projected_ref[...]))

    return call(
        kernel,
        index,
        (NP,),
        [pl.BlockSpec((group, quarter), lambda p, t: (p, 0))] * NT
        + [
            pl.BlockSpec((NT * quarter, part), lambda p, t: (0, 0)),
            pl.BlockSpec((own, part), lambda p, t: (p, 0)),
        ],
        pl.BlockSpec((1, group + 2 * own, part), lambda p, t: (p, 0, 0)),
        jax.ShapeDtypeStruct((NP, group + 2 * own, part), BF16),
        [],
        (2 * NP * group * NT * quarter * part, 2 * NP * group * (NT * quarter + part)),
        24,
        *pieces,
        step_dir,
        projected,
    )


def moments_of(first_moment, second_moment, projected):
    new_first = 0.9 * first_moment + 0.1 * projected
    new_second = 0.95 * second_moment + 0.05 * projected * projected
    return new_first, new_second


def local(tokens, grad_out, basis, first_moment, second_moment):
    rows, rank = basis.shape
    quarter = rank // NT
    group = NT * rows
    columns = grad_out.shape[1]
    own = rank // (NZ * NP)
    part = columns // NP
    index = (NC * lax.axis_index("yh") + lax.axis_index("core")).astype(jnp.int32).reshape(1)

    pieces = basis.reshape(rows, NT, quarter).transpose(1, 0, 2)
    pieces = jnp.broadcast_to(pieces[None], (NZ, NT, rows, quarter))
    line = exchange(pieces.reshape(NZ * NT, rows, quarter), ("z",) + TENSOR)
    blocks, beside = plane_blocks(line.reshape(NZ, group, quarter))
    tokens, beside = lax.optimization_barrier((tokens, beside))
    (tokens,) = loaded(tokens)
    coords = peers(coordinates(tokens, blocks))

    partial = partial_sums(index, coords, grad_out, first_moment, second_moment)
    partial, first_part, second_part = plane_sums(index, exchange(partial, PLANE), own)

    blocks, partial = lax.optimization_barrier((blocks, partial))
    rows_here = lax.dynamic_index_in_dim(blocks, lax.axis_index("z"), axis=0, keepdims=False)
    rows_here = peers(rows_here.reshape(NP * group, quarter))

    partial = exchange(partial.reshape(NZ, NP * own, part), ("z",))
    projected = jnp.sum(partial.astype(F32), axis=0)
    new_first, new_second = moments_of(first_part, second_part, projected)
    first_fix = 1.0 - 0.9**STEP
    second_fix = 1.0 - 0.95**STEP
    step_dir = (new_first / first_fix / (jnp.sqrt(new_second / second_fix) + 1e-08)).astype(BF16)
    step_dir = gather(step_dir, ("z",), NZ).reshape(rank, part)

    back = update_blocks(index, rows_here, step_dir, projected, own)
    back = exchange(back, PLANE).transpose(1, 0, 2).reshape(group + 2 * own, columns)
    projected = back[group : group + own].astype(F32) + back[group + own :].astype(F32)
    new_first, new_second = moments_of(first_moment, second_moment, projected)
    return (back[:group], new_first, new_second)


def solution(mesh):
    fine = Mesh(mesh.devices.reshape(NZ, NX, NYL, NYH, NC), AXES)
    placed = (
        P(DP, None),
        P(DP, TENSOR),
        P(DP + TENSOR, None),
        P(DP, TENSOR),
        P(DP, TENSOR),
    )
    return jax.shard_map(
        local,
        mesh=fine,
        in_specs=placed,
        out_specs=(P(DP, TENSOR), P(DP, TENSOR), P(DP, TENSOR)),
        check_vma=False,
    )
```

```python
import jax
import jax.numpy as jnp
from jax import lax
from jax.experimental import pallas as pl
from jax.experimental.pallas import tpu as pltpu
from jax.sharding import Mesh, PartitionSpec as P

STEP = 20
AXES = ("z", "x", "yl", "yh", "core")
DP = ("z", "x", "yl")
TENSOR = ("yh", "core")
PLANE = ("x", "yl")
NZ, NX, NYL, NYH, NC = 8, 4, 2, 2, 2
NP = NX * NYL
NT = NYH * NC
PAIR = 2
MIB = 1024 * 1024
F32, BF16 = jnp.float32, jnp.bfloat16


def exchange(blocks, axes):
    return lax.all_to_all(blocks, axes, 0, 0, tiled=True)


def gather(block, axes, members):
    return exchange(jnp.broadcast_to(block[None], (members,) + block.shape), axes)


def swap(block, axis):
    return lax.ppermute(block, axis, ((0, 1), (1, 0)))


def peers(block):
    far = swap(block, "yh")
    return block, swap(block, "core"), far, swap(far, "core")


def halves(value):
    high = value.astype(BF16)
    return high, (value - high.astype(F32)).astype(BF16)


def call(kernel, index, grid, in_specs, out_specs, out_shape, scratch, cost, limit, *args):
    return pl.pallas_call(
        kernel,
        grid_spec=pltpu.PrefetchScalarGridSpec(
            num_scalar_prefetch=1,
            grid=grid,
            in_specs=in_specs,
            out_specs=out_specs,
            scratch_shapes=scratch,
        ),
        out_shape=out_shape,
        compiler_params=pltpu.CompilerParams(vmem_limit_bytes=limit * MIB),
        cost_estimate=pl.CostEstimate(flops=cost[0], bytes_accessed=cost[1], transcendentals=0),
    )(index, *args)


def along(block, shift):
    return lax.ppermute(block, "x", [(i, (i + shift) % NX) for i in range(NX)])


def plane_blocks(line):
    half = line.shape[0] // 2
    beside, left, right = swap(line, "yl"), along(line, 1), along(line, -1)
    far_low, far_high = along(left[:half], 1), along(right[half:], -1)
    beside_left, beside_right = along(beside, 1), along(beside, -1)
    pieces = (
        (line, 0, 0, 0),
        (beside, 0, 1, 0),
        (left, NX - 1, 0, 0),
        (right, 1, 0, 0),
        (far_low, 2, 0, 0),
        (far_high, 2, 0, half),
        (beside_left, NX - 1, 1, 0),
        (beside_right, 1, 1, 0),
        (swap(far_low, "yl"), 2, 1, 0),
        (swap(far_high, "yl"), 2, 1, half),
    )
    x, yl = lax.axis_index("x"), lax.axis_index("yl")
    blocks = jnp.zeros((line.shape[0], NP) + line.shape[1:], BF16)
    for piece, dx, dy, start in pieces:
        member = ((x + dx) & (NX - 1)) * NYL + (yl ^ dy)
        blocks = lax.dynamic_update_slice(blocks, piece[:, None], (start, member, 0, 0))
    return blocks


def loaded(*arrays):
    count = len(arrays)

    def kernel(*refs):
        sources, outs, arrived = refs[:count], refs[count:-1], refs[-1]
        copies = [
            pltpu.make_async_copy(sources[k], outs[k], arrived.at[k]) for k in range(count)
        ]
        for copy in copies:
            copy.start()
        for copy in copies:
            copy.wait()

    return pl.pallas_call(
        kernel,
        in_specs=[pl.BlockSpec(memory_space=pltpu.HBM)] * count,
        out_specs=[pl.BlockSpec(memory_space=pltpu.VMEM)] * count,
        out_shape=[jax.ShapeDtypeStruct(array.shape, array.dtype) for array in arrays],
        scratch_shapes=[pltpu.SemaphoreType.DMA((count,))],
        compiler_params=pltpu.CompilerParams(vmem_limit_bytes=40 * MIB),
        cost_estimate=pl.CostEstimate(
            flops=0, bytes_accessed=4 * sum(array.size for array in arrays), transcendentals=0
        ),
    )(*arrays)


def coordinates(tokens, blocks):
    part = blocks.reshape(tokens.shape[1], blocks.shape[3])
    return jnp.dot(tokens, part, preferred_element_type=F32).astype(BF16).T


def partial_sums(index, coords, grad_out, first_moment, second_moment):
    quarter, count = coords[0].shape
    rank, columns = NT * quarter, grad_out.shape[1]
    own, part = first_moment.shape[0], columns // NP
    rows = rank + 4 * own

    def kernel(index_ref, *refs):
        pieces, (grad_ref, first_ref, second_ref, out) = refs[:NT], refs[NT:]
        for j in range(PAIR):
            here = slice(j * part, (j + 1) * part)
            for k in range(NT):
                start = pl.multiple_of((index_ref[0] ^ k) * quarter, quarter)
                out[j, pl.ds(start, quarter), :] = jnp.dot(
                    pieces[k][...], grad_ref[:, here], preferred_element_type=F32
                ).astype(BF16)
            out[j, rank : rank + 2 * own, :] = jnp.concatenate(halves(first_ref[:, here]))
            out[j, rank + 2 * own :, :] = jnp.concatenate(halves(second_ref[:, here]))

    return call(
        kernel,
        index,
        (NP // PAIR,),
        [pl.BlockSpec((quarter, count), lambda p, t: (0, 0))] * NT
        + [pl.BlockSpec((count, PAIR * part), lambda p, t: (0, p))]
        + [pl.BlockSpec((own, PAIR * part), lambda p, t: (0, p))] * 2,
        pl.BlockSpec((PAIR, rows, part), lambda p, t: (p, 0, 0)),
        jax.ShapeDtypeStruct((NP, rows, part), BF16),
        [],
        (2 * rank * count * columns, 2 * columns * (count + rows)),
        24,
        *coords,
        grad_out,
        first_moment,
        second_moment,
    )


def plane_sums(index, received, own):
    members, rows, part = received.shape
    rank = rows - 4 * own
    step = rank // 4

    def kernel(index_ref, sums_ref, moments_ref, out, first, second):
        total = sums_ref[0].astype(F32)
        for source in range(1, members):
            total += sums_ref[source].astype(F32)
        out[...] = total.astype(BF16)

        @pl.when(pl.program_id(0) == 0)
        def _():
            for source in range(members):
                block = moments_ref[source].astype(F32)
                here = slice(source * own, (source + 1) * own)
                first[here, :] = block[:own] + block[own : 2 * own]
                second[here, :] = block[2 * own : 3 * own] + block[3 * own :]

    return call(
        kernel,
        index,
        (4,),
        [
            pl.BlockSpec((members, step, part), lambda i, t: (0, i, 0)),
            pl.BlockSpec((members, 4 * own, part), lambda i, t: (0, rank // (4 * own), 0)),
        ],
        [
            pl.BlockSpec((step, part), lambda i, t: (i, 0)),
            pl.BlockSpec((members * own, part), lambda i, t: (0, 0)),
            pl.BlockSpec((members * own, part), lambda i, t: (0, 0)),
        ],
        [
            jax.ShapeDtypeStruct((rank, part), BF16),
            jax.ShapeDtypeStruct((members * own, part), F32),
            jax.ShapeDtypeStruct((members * own, part), F32),
        ],
        [],
        (members * rank * part, 2 * members * rows * part),
        24,
        received,
        received,
    )


def update_blocks(index, pieces, step_dir, projected, own):
    quarter = pieces[0].shape[1]
    group = pieces[0].shape[0] // NP
    part = step_dir.shape[1]

    def kernel(index_ref, *refs):
        blocks, (step_ref, projected_ref, out) = refs[:NT], refs[NT:]
        total = 0.0
        for k in range(NT):
            start = pl.multiple_of((index_ref[0] ^ k) * quarter, quarter)
            total += jnp.dot(
                blocks[k][...], step_ref[pl.ds(start, quarter), :], preferred_element_type=F32
            )
        for j in range(PAIR):
            out[j, :group, :] = total[j * group : (j + 1) * group].astype(BF16)
            out[j, group:, :] = jnp.concatenate(halves(projected_ref[j * own : (j + 1) * own, :]))

    return call(
        kernel,
        index,
        (NP // PAIR,),
        [pl.BlockSpec((PAIR * group, quarter), lambda p, t: (p, 0))] * NT
        + [
            pl.BlockSpec((NT * quarter, part), lambda p, t: (0, 0)),
            pl.BlockSpec((PAIR * own, part), lambda p, t: (p, 0)),
        ],
        pl.BlockSpec((PAIR, group + 2 * own, part), lambda p, t: (p, 0, 0)),
        jax.ShapeDtypeStruct((NP, group + 2 * own, part), BF16),
        [],
        (2 * NP * group * NT * quarter * part, 2 * NP * group * (NT * quarter + part)),
        24,
        *pieces,
        step_dir,
        projected,
    )


def outputs(index, back, first_moment, second_moment):
    own, columns = first_moment.shape
    members, rows, part = back.shape
    group, count = rows - 2 * own, members // 2
    wide = count * part

    def kernel(index_ref, back_ref, first_ref, second_ref, update, new_first, new_second):
        for j in range(count):
            here = slice(j * part, (j + 1) * part)
            update[:, here] = back_ref[j, :group, :]
            terms = back_ref[j, group:, :].astype(F32)
            new_first[:, here], new_second[:, here] = moments_of(
                first_ref[:, here], second_ref[:, here], terms[:own] + terms[own:]
            )

    moment = pl.BlockSpec((own, wide), lambda p, t: (0, p))
    return call(
        kernel,
        index,
        (2,),
        [pl.BlockSpec((count, rows, part), lambda p, t: (p, 0, 0)), moment, moment],
        [pl.BlockSpec((group, wide), lambda p, t: (0, p)), moment, moment],
        [
            jax.ShapeDtypeStruct((group, columns), BF16),
            jax.ShapeDtypeStruct((own, columns), F32),
            jax.ShapeDtypeStruct((own, columns), F32),
        ],
        [],
        (8 * own * columns, 4 * columns * (rows + 4 * own)),
        16,
        back,
        first_moment,
        second_moment,
    )


def moments_of(first_moment, second_moment, projected):
    new_first = 0.9 * first_moment + 0.1 * projected
    new_second = 0.95 * second_moment + 0.05 * projected * projected
    return new_first, new_second


def local(tokens, grad_out, basis, first_moment, second_moment):
    rows, rank = basis.shape
    quarter = rank // NT
    group = NT * rows
    columns = grad_out.shape[1]
    own = rank // (NZ * NP)
    part = columns // NP
    index = (NC * lax.axis_index("yh") + lax.axis_index("core")).astype(jnp.int32).reshape(1)

    pieces = basis.reshape(rows, NT, quarter).transpose(1, 0, 2)
    pieces = jnp.broadcast_to(pieces[None], (NZ, NT, rows, quarter))
    line = exchange(pieces.reshape(NZ * NT, rows, quarter), ("z",) + TENSOR)
    tokens, line = lax.optimization_barrier((tokens, line))
    blocks = plane_blocks(line.reshape(NZ, group, quarter))
    (tokens,) = loaded(tokens)
    coords = peers(coordinates(tokens, blocks))

    partial = partial_sums(index, coords, grad_out, first_moment, second_moment)
    partial, first_part, second_part = plane_sums(index, exchange(partial, PLANE), own)

    blocks, partial = lax.optimization_barrier((blocks, partial))
    rows_here = lax.dynamic_index_in_dim(blocks, lax.axis_index("z"), axis=0, keepdims=False)
    rows_here = peers(rows_here.reshape(NP * group, quarter))

    partial = exchange(partial.reshape(NZ, NP * own, part), ("z",))
    projected = jnp.sum(partial.astype(F32), axis=0)
    new_first, new_second = moments_of(first_part, second_part, projected)
    first_fix = 1.0 - 0.9**STEP
    second_fix = 1.0 - 0.95**STEP
    step_dir = (new_first / first_fix / (jnp.sqrt(new_second / second_fix) + 1e-08)).astype(BF16)
    step_dir = gather(step_dir, ("z",), NZ).reshape(rank, part)

    back = update_blocks(index, rows_here, step_dir, projected, own)
    update, new_first, new_second = outputs(
        index, exchange(back, PLANE), first_moment, second_moment
    )
    return (update, new_first, new_second)


def solution(mesh):
    fine = Mesh(mesh.devices.reshape(NZ, NX, NYL, NYH, NC), AXES)
    placed = (
        P(DP, None),
        P(DP, TENSOR),
        P(DP + TENSOR, None),
        P(DP, TENSOR),
        P(DP, TENSOR),
    )
    return jax.shard_map(
        local,
        mesh=fine,
        in_specs=placed,
        out_specs=(P(DP, TENSOR), P(DP, TENSOR), P(DP, TENSOR)),
        check_vma=False,
    )
```

```python
import jax
import jax.numpy as jnp
from jax import lax
from jax.experimental import pallas as pl
from jax.experimental.pallas import tpu as pltpu
from jax.sharding import Mesh, PartitionSpec as P

STEP = 20
AXES = ("z", "x", "yl", "yh", "core")
DP = ("z", "x", "yl")
TENSOR = ("yh", "core")
PLANE = ("x", "yl")
NZ, NX, NYL, NYH, NC = 8, 4, 2, 2, 2
NP = NX * NYL
NT = NYH * NC
PAIR = 4
MIB = 1024 * 1024
F32, BF16 = jnp.float32, jnp.bfloat16


def exchange(blocks, axes):
    return lax.all_to_all(blocks, axes, 0, 0, tiled=True)


def gather(block, axes, members):
    return exchange(jnp.broadcast_to(block[None], (members,) + block.shape), axes)


def swap(block, axis):
    return lax.ppermute(block, axis, ((0, 1), (1, 0)))


def peers(block):
    far = swap(block, "yh")
    return block, swap(block, "core"), far, swap(far, "core")


def halves(value):
    high = value.astype(BF16)
    return high, (value - high.astype(F32)).astype(BF16)


def call(kernel, index, grid, in_specs, out_specs, out_shape, scratch, cost, limit, *args):
    return pl.pallas_call(
        kernel,
        grid_spec=pltpu.PrefetchScalarGridSpec(
            num_scalar_prefetch=1,
            grid=grid,
            in_specs=in_specs,
            out_specs=out_specs,
            scratch_shapes=scratch,
        ),
        out_shape=out_shape,
        compiler_params=pltpu.CompilerParams(vmem_limit_bytes=limit * MIB),
        cost_estimate=pl.CostEstimate(flops=cost[0], bytes_accessed=cost[1], transcendentals=0),
    )(index, *args)


def along(block, shift):
    return lax.ppermute(block, "x", [(i, (i + shift) % NX) for i in range(NX)])


def plane_blocks(line):
    half = line.shape[0] // 2
    beside, left, right = swap(line, "yl"), along(line, 1), along(line, -1)
    far_low, far_high = along(left[:half], 1), along(right[half:], -1)
    beside_left, beside_right = along(beside, 1), along(beside, -1)
    pieces = (
        (line, 0, 0, 0),
        (beside, 0, 1, 0),
        (left, NX - 1, 0, 0),
        (right, 1, 0, 0),
        (far_low, 2, 0, 0),
        (far_high, 2, 0, half),
        (beside_left, NX - 1, 1, 0),
        (beside_right, 1, 1, 0),
        (swap(far_low, "yl"), 2, 1, 0),
        (swap(far_high, "yl"), 2, 1, half),
    )
    x, yl = lax.axis_index("x"), lax.axis_index("yl")
    blocks = jnp.zeros((line.shape[0], NP) + line.shape[1:], BF16)
    for piece, dx, dy, start in pieces:
        member = ((x + dx) & (NX - 1)) * NYL + (yl ^ dy)
        blocks = lax.dynamic_update_slice(blocks, piece[:, None], (start, member, 0, 0))
    return blocks


def loaded(*arrays):
    count = len(arrays)

    def kernel(*refs):
        sources, outs, arrived = refs[:count], refs[count:-1], refs[-1]
        copies = [
            pltpu.make_async_copy(sources[k], outs[k], arrived.at[k]) for k in range(count)
        ]
        for copy in copies:
            copy.start()
        for copy in copies:
            copy.wait()

    return pl.pallas_call(
        kernel,
        in_specs=[pl.BlockSpec(memory_space=pltpu.HBM)] * count,
        out_specs=[pl.BlockSpec(memory_space=pltpu.VMEM)] * count,
        out_shape=[jax.ShapeDtypeStruct(array.shape, array.dtype) for array in arrays],
        scratch_shapes=[pltpu.SemaphoreType.DMA((count,))],
        compiler_params=pltpu.CompilerParams(vmem_limit_bytes=40 * MIB),
        cost_estimate=pl.CostEstimate(
            flops=0, bytes_accessed=4 * sum(array.size for array in arrays), transcendentals=0
        ),
    )(*arrays)


def coordinates(tokens, blocks):
    part = blocks.reshape(tokens.shape[1], blocks.shape[3])
    return jnp.dot(tokens, part, preferred_element_type=F32).astype(BF16).T


def partial_sums(index, coords, grad_out, first_moment, second_moment):
    quarter, count = coords[0].shape
    rank, columns = NT * quarter, grad_out.shape[1]
    own, part = first_moment.shape[0], columns // NP
    rows = rank + 4 * own

    def kernel(index_ref, *refs):
        pieces, (grad_ref, first_ref, second_ref, out) = refs[:NT], refs[NT:]
        for j in range(PAIR):
            here = slice(j * part, (j + 1) * part)
            for k in range(NT):
                start = pl.multiple_of((index_ref[0] ^ k) * quarter, quarter)
                out[j, pl.ds(start, quarter), :] = jnp.dot(
                    pieces[k][...], grad_ref[:, here], preferred_element_type=F32
                ).astype(BF16)
            out[j, rank : rank + 2 * own, :] = jnp.concatenate(halves(first_ref[:, here]))
            out[j, rank + 2 * own :, :] = jnp.concatenate(halves(second_ref[:, here]))

    return call(
        kernel,
        index,
        (NP // PAIR,),
        [pl.BlockSpec((quarter, count), lambda p, t: (0, 0))] * NT
        + [pl.BlockSpec((count, PAIR * part), lambda p, t: (0, p))]
        + [pl.BlockSpec((own, PAIR * part), lambda p, t: (0, p))] * 2,
        pl.BlockSpec((PAIR, rows, part), lambda p, t: (p, 0, 0)),
        jax.ShapeDtypeStruct((NP, rows, part), BF16),
        [],
        (2 * rank * count * columns, 2 * columns * (count + rows)),
        24,
        *coords,
        grad_out,
        first_moment,
        second_moment,
    )


def plane_sums(index, received, own):
    members, rows, part = received.shape
    rank = rows - 4 * own
    step = rank // 2

    def kernel(index_ref, sums_ref, moments_ref, out, first, second):
        total = sums_ref[0].astype(F32)
        for source in range(1, members):
            total += sums_ref[source].astype(F32)
        out[...] = total.astype(BF16)

        @pl.when(pl.program_id(0) == 0)
        def _():
            for source in range(members):
                block = moments_ref[source].astype(F32)
                here = slice(source * own, (source + 1) * own)
                first[here, :] = block[:own] + block[own : 2 * own]
                second[here, :] = block[2 * own : 3 * own] + block[3 * own :]

    return call(
        kernel,
        index,
        (2,),
        [
            pl.BlockSpec((members, step, part), lambda i, t: (0, i, 0)),
            pl.BlockSpec((members, 4 * own, part), lambda i, t: (0, rank // (4 * own), 0)),
        ],
        [
            pl.BlockSpec((step, part), lambda i, t: (i, 0)),
            pl.BlockSpec((members * own, part), lambda i, t: (0, 0)),
            pl.BlockSpec((members * own, part), lambda i, t: (0, 0)),
        ],
        [
            jax.ShapeDtypeStruct((rank, part), BF16),
            jax.ShapeDtypeStruct((members * own, part), F32),
            jax.ShapeDtypeStruct((members * own, part), F32),
        ],
        [],
        (members * rank * part, 2 * members * rows * part),
        24,
        received,
        received,
    )


def update_blocks(index, pieces, step_dir, projected, own):
    quarter = pieces[0].shape[1]
    group = pieces[0].shape[0] // NP
    part = step_dir.shape[1]

    def kernel(index_ref, *refs):
        blocks, (step_ref, projected_ref, out) = refs[:NT], refs[NT:]
        total = 0.0
        for k in range(NT):
            start = pl.multiple_of((index_ref[0] ^ k) * quarter, quarter)
            total += jnp.dot(
                blocks[k][...], step_ref[pl.ds(start, quarter), :], preferred_element_type=F32
            )
        for j in range(PAIR):
            out[j, :group, :] = total[j * group : (j + 1) * group].astype(BF16)
            out[j, group:, :] = jnp.concatenate(halves(projected_ref[j * own : (j + 1) * own, :]))

    return call(
        kernel,
        index,
        (NP // PAIR,),
        [pl.BlockSpec((PAIR * group, quarter), lambda p, t: (p, 0))] * NT
        + [
            pl.BlockSpec((NT * quarter, part), lambda p, t: (0, 0)),
            pl.BlockSpec((PAIR * own, part), lambda p, t: (p, 0)),
        ],
        pl.BlockSpec((PAIR, group + 2 * own, part), lambda p, t: (p, 0, 0)),
        jax.ShapeDtypeStruct((NP, group + 2 * own, part), BF16),
        [],
        (2 * NP * group * NT * quarter * part, 2 * NP * group * (NT * quarter + part)),
        24,
        *pieces,
        step_dir,
        projected,
    )


def outputs(index, back, first_moment, second_moment):
    own, columns = first_moment.shape
    members, rows, part = back.shape
    group, count = rows - 2 * own, members // 2
    wide = count * part

    def kernel(index_ref, back_ref, first_ref, second_ref, update, new_first, new_second):
        for j in range(count):
            here = slice(j * part, (j + 1) * part)
            update[:, here] = back_ref[j, :group, :]
            terms = back_ref[j, group:, :].astype(F32)
            new_first[:, here], new_second[:, here] = moments_of(
                first_ref[:, here], second_ref[:, here], terms[:own] + terms[own:]
            )

    moment = pl.BlockSpec((own, wide), lambda p, t: (0, p))
    return call(
        kernel,
        index,
        (2,),
        [pl.BlockSpec((count, rows, part), lambda p, t: (p, 0, 0)), moment, moment],
        [pl.BlockSpec((group, wide), lambda p, t: (0, p)), moment, moment],
        [
            jax.ShapeDtypeStruct((group, columns), BF16),
            jax.ShapeDtypeStruct((own, columns), F32),
            jax.ShapeDtypeStruct((own, columns), F32),
        ],
        [],
        (8 * own * columns, 4 * columns * (rows + 4 * own)),
        16,
        back,
        first_moment,
        second_moment,
    )


def moments_of(first_moment, second_moment, projected):
    new_first = 0.9 * first_moment + 0.1 * projected
    new_second = 0.95 * second_moment + 0.05 * projected * projected
    return new_first, new_second


def local(tokens, grad_out, basis, first_moment, second_moment):
    rows, rank = basis.shape
    quarter = rank // NT
    group = NT * rows
    columns = grad_out.shape[1]
    own = rank // (NZ * NP)
    part = columns // NP
    index = (NC * lax.axis_index("yh") + lax.axis_index("core")).astype(jnp.int32).reshape(1)

    pieces = basis.reshape(rows, NT, quarter).transpose(1, 0, 2)
    pieces = jnp.broadcast_to(pieces[None], (NZ, NT, rows, quarter))
    line = exchange(pieces.reshape(NZ * NT, rows, quarter), ("z",) + TENSOR)
    tokens, line = lax.optimization_barrier((tokens, line))
    blocks = plane_blocks(line.reshape(NZ, group, quarter))
    (tokens,) = loaded(tokens)
    coords = peers(coordinates(tokens, blocks))

    partial = partial_sums(index, coords, grad_out, first_moment, second_moment)
    partial, first_part, second_part = plane_sums(index, exchange(partial, PLANE), own)

    blocks, partial = lax.optimization_barrier((blocks, partial))
    rows_here = lax.dynamic_index_in_dim(blocks, lax.axis_index("z"), axis=0, keepdims=False)
    rows_here = peers(rows_here.reshape(NP * group, quarter))

    partial = exchange(partial.reshape(NZ, NP * own, part), ("z",))
    projected = jnp.sum(partial.astype(F32), axis=0)
    new_first, new_second = moments_of(first_part, second_part, projected)
    first_fix = 1.0 - 0.9**STEP
    second_fix = 1.0 - 0.95**STEP
    step_dir = (new_first / first_fix / (jnp.sqrt(new_second / second_fix) + 1e-08)).astype(BF16)
    step_dir = gather(step_dir, ("z",), NZ).reshape(rank, part)

    back = update_blocks(index, rows_here, step_dir, projected, own)
    update, new_first, new_second = outputs(
        index, exchange(back, PLANE), first_moment, second_moment
    )
    return (update, new_first, new_second)


def solution(mesh):
    fine = Mesh(mesh.devices.reshape(NZ, NX, NYL, NYH, NC), AXES)
    placed = (
        P(DP, None),
        P(DP, TENSOR),
        P(DP + TENSOR, None),
        P(DP, TENSOR),
        P(DP, TENSOR),
    )
    return jax.shard_map(
        local,
        mesh=fine,
        in_specs=placed,
        out_specs=(P(DP, TENSOR), P(DP, TENSOR), P(DP, TENSOR)),
        check_vma=False,
    )
```
